32 devices in a mesh: dp: 4 (over z), zero: 8 (over y, x, core).
Axes of the slice: x: 2, y: 2, z: 4, core: 2. Of those that a mesh axis runs over, the one named last changes fastest.
Arguments:
- images: bfloat16 [160, 197, 768], P(('dp', 'zero')), may hold values from -6 to 6
- cotangent: bfloat16 [160, 197, 768], P(('dp', 'zero')), may hold values from -6 to 6
- counts: int32 [32], P(('dp', 'zero')), may hold values from 3 to 5, as said below
- master_qkv: float32 [768, 2304], P('zero'), may hold values from -0.21875 to 0.21875
- master_proj: float32 [768, 768], P('zero'), may hold values from -0.875 to 0.875
- master_fc1: float32 [768, 3072], P('zero'), may hold values from -0.21875 to 0.21875
- master_fc2: float32 [3072, 768], P('zero'), may hold values from -0.109375 to 0.109375
- master_vectors: float32 [12, 768], P(None, 'zero'), may hold values from -1 to 1.6
- first_qkv: float32 [768, 2304], P('zero'), may hold values from -56 to 56
- first_proj: float32 [768, 768], P('zero'), may hold values from -56 to 56
- first_fc1: float32 [768, 3072], P('zero'), may hold values from -56 to 56
- first_fc2: float32 [3072, 768], P('zero'), may hold values from -56 to 56
- first_vectors: float32 [12, 768], P(None, 'zero'), may hold values from -112 to 112
- second_qkv: float32 [768, 2304], P('zero'), may hold values from 7.88 to 31.52
- second_proj: float32 [768, 768], P('zero'), may hold values from 7.88 to 31.52
- second_fc1: float32 [768, 3072], P('zero'), may hold values from 7.88 to 31.52
- second_fc2: float32 [3072, 768], P('zero'), may hold values from 7.88 to 31.52
- second_vectors: float32 [12, 768], P(None, 'zero'), may hold values from 31.52 to 126.08
Outputs:
- block_out: bfloat16 [160, 197, 768], P(('dp', 'zero'))
- grad_input: float32 [160, 197, 768], P(('dp', 'zero'))
- grad_qkv: float32 [768, 2304], P('zero')
- grad_proj: float32 [768, 768], P('zero')
- grad_fc1: float32 [768, 3072], P('zero')
- grad_fc2: float32 [3072, 768], P('zero')
- grad_vectors: float32 [12, 768], P(None, 'zero')
- next_qkv: float32 [768, 2304], P('zero')
- next_proj: float32 [768, 768], P('zero')
- next_fc1: float32 [768, 3072], P('zero')
- next_fc2: float32 [3072, 768], P('zero')
- next_vectors: float32 [12, 768], P(None, 'zero')
- next_first_qkv: float32 [768, 2304], P('zero')
- next_first_proj: float32 [768, 768], P('zero')
- next_first_fc1: float32 [768, 3072], P('zero')
- next_first_fc2: float32 [3072, 768], P('zero')
- next_first_vectors: float32 [12, 768], P(None, 'zero')
- next_second_qkv: float32 [768, 2304], P('zero')
- next_second_proj: float32 [768, 768], P('zero')
- next_second_fc1: float32 [768, 3072], P('zero')
- next_second_fc2: float32 [3072, 768], P('zero')
- next_second_vectors: float32 [12, 768], P(None, 'zero')
The draws below stay inside these ranges and needn't reach their ends.
Inputs may be any that keep to these rules, and one draw needn't show every extreme that they name: `counts`: in every draw some device has 5 live slots and some has 3.
All inputs are finite; a program needn't handle non-finite values.
Results may differ from the reference program's by a relative error of at most 0.012.
The reference program's roundings to bfloat16 on the way count: a program that leaves them out, or rounds other values in their place, can miss the bound.
Values may be sent and summed in bfloat16 or wider, within the bound.
A program may use at most 192 MiB of HBM per device.

```python
import math
import jax
import jax.numpy as jnp
from jax import lax

D = 768
HEADS = 12
HEAD_DIM = 64
FF = 3072
SEQ = 197
CAP = 5
STEP = 10
GROUPS = 32
SLOTS_ALL = 160
VEC_ROWS = 12


def draw_counts(key, part):
    key = jax.random.fold_in(key, 11)
    key_base, key_high, key_low = jax.random.split(key, 3)
    least_count = CAP - CAP // 2
    drawn_counts = jax.random.randint(key_base, (GROUPS,), least_count, CAP + 1)
    high_index = jax.random.randint(key_high, (), 0, GROUPS)
    low_index = (high_index + 1 + jax.random.randint(key_low, (), 0, GROUPS - 1)) % GROUPS
    return drawn_counts.at[high_index].set(CAP).at[low_index].set(least_count).astype(jnp.int32)


def draw_master_vectors(key, part):
    key = jax.random.fold_in(key, 23)
    key_bias, key_gain = jax.random.split(key)
    row_count = 8 + FF // D
    biases = jnp.clip(jax.random.normal(key_bias, (row_count, D), jnp.float32), -5.0, 5.0) * 0.2
    gains = jax.random.uniform(key_gain, (row_count, D), jnp.float32, 0.5, 1.5)
    row_index = jnp.arange(row_count)
    is_gain = (row_index == 0) | (row_index == 5)
    return jnp.where(is_gain[:, None], gains, biases)


def steps_of(key, extent, shards, smallest, high):
    factor_of = 1.0
    for position, blocks in shards:
        steps = jax.random.uniform(jax.random.fold_in(jax.random.fold_in(key, 6), position), (blocks,), jnp.float32, smallest / len(shards), high / len(shards))
        factor_of = factor_of * jnp.repeat(jnp.exp(steps), extent[position] // blocks).reshape((-1,) + (1,) * (len(extent) - 1 - position))
    return factor_of


def gaussian(own_key, dims, scale, most, cuts=(), kind=jnp.bfloat16):
    values = jax.random.normal(own_key, dims, jnp.float32) * scale
    if len(cuts) > 0:
        values = steps_of(own_key, dims, cuts, -0.22, 0.18) * values
    return jnp.clip(values, min=-most, max=most).astype(kind)


def setup_inputs(seed: int = 0) -> dict:
    splits = jax.random.split(jax.random.key(seed), 19)
    images = gaussian(splits[0], (SLOTS_ALL, SEQ, D), 1.0, 6.0, ((0, 32),))
    cotangent = gaussian(splits[1], (SLOTS_ALL, SEQ, D), 1.0, 6.0, ((0, 32),))
    counts = draw_counts(jax.random.fold_in(splits[18], 71), 0)
    master_qkv = gaussian(splits[3], (D, 3 * D), D ** -0.5, 0.21875, ((0, 8),), jnp.float32)
    master_proj = gaussian(splits[4], (D, D), (D // 16) ** -0.5, 0.875, ((0, 8),), jnp.float32)
    master_fc1 = gaussian(splits[5], (D, FF), D ** -0.5, 0.21875, ((0, 8),), jnp.float32)
    master_fc2 = gaussian(splits[6], (FF, D), FF ** -0.5, 0.109375, ((0, 8),), jnp.float32)
    master_vectors = draw_master_vectors(jax.random.fold_in(splits[18], 71), 0)
    first_qkv = gaussian(splits[8], (D, 3 * D), (0.055 * (GROUPS * CAP * SEQ) ** 0.5), 56.0, ((0, 8),), jnp.float32)
    first_proj = gaussian(splits[9], (D, D), (0.055 * (GROUPS * CAP * SEQ) ** 0.5), 56.0, ((0, 8),), jnp.float32)
    first_fc1 = gaussian(splits[10], (D, FF), (0.055 * (GROUPS * CAP * SEQ) ** 0.5), 56.0, ((0, 8),), jnp.float32)
    first_fc2 = gaussian(splits[11], (FF, D), (0.055 * (GROUPS * CAP * SEQ) ** 0.5), 56.0, ((0, 8),), jnp.float32)
    first_vectors = gaussian(splits[12], (VEC_ROWS, D), (0.11 * (GROUPS * CAP * SEQ) ** 0.5), 112.0, ((1, 8),), jnp.float32)
    second_qkv = jnp.clip(jnp.exp(math.log(31.52) - 1.3862944 * jax.random.uniform(splits[13], (D, 3 * D), jnp.float32) ** steps_of(splits[13], (D, 3 * D), ((0, 8),), -0.2, 0.2)), 7.88, 31.52)
    second_proj = jnp.clip(jnp.exp(math.log(31.52) - 1.3862944 * jax.random.uniform(splits[14], (D, D), jnp.float32) ** steps_of(splits[14], (D, D), ((0, 8),), -0.2, 0.2)), 7.88, 31.52)
    second_fc1 = jnp.clip(jnp.exp(math.log(31.52) - 1.3862944 * jax.random.uniform(splits[15], (D, FF), jnp.float32) ** steps_of(splits[15], (D, FF), ((0, 8),), -0.2, 0.2)), 7.88, 31.52)
    second_fc2 = jnp.clip(jnp.exp(math.log(31.52) - 1.3862944 * jax.random.uniform(splits[16], (FF, D), jnp.float32) ** steps_of(splits[16], (FF, D), ((0, 8),), -0.2, 0.2)), 7.88, 31.52)
    second_vectors = jnp.clip(jnp.exp(math.log(126.08) - 1.3862944 * jax.random.uniform(splits[17], (VEC_ROWS, D), jnp.float32) ** steps_of(splits[17], (VEC_ROWS, D), ((1, 8),), -0.2, 0.2)), 31.52, 126.08)
    return dict(images=images, cotangent=cotangent, counts=counts, master_qkv=master_qkv, master_proj=master_proj, master_fc1=master_fc1, master_fc2=master_fc2, master_vectors=master_vectors, first_qkv=first_qkv, first_proj=first_proj, first_fc1=first_fc1, first_fc2=first_fc2, first_vectors=first_vectors, second_qkv=second_qkv, second_proj=second_proj, second_fc1=second_fc1, second_fc2=second_fc2, second_vectors=second_vectors)


@jax.custom_vjp
def low(v):
    return lax.optimization_barrier(v.astype(jnp.bfloat16)).astype(jnp.float32)

@jax.custom_vjp
def low_back(v):
    return v

def low_keep(v):
    return (low(v), None)

def low_pass(kept, grad):
    return (grad,)

def back_keep(v):
    return (v, None)

def back_low(kept, grad):
    return (low(grad),)
low.defvjp(low_keep, low_pass)
low_back.defvjp(back_keep, back_low)
LN_EPS = 1e-06
BETA_ONE = 0.9
BETA_TWO = 0.999
ADAM_EPS = 1e-08
RATE_MATRIX = 0.05
RATE_VECTOR = 0.2
DECAY_MATRIX = 0.05

def product(left_side, right_side):
    return jnp.matmul(left_side, right_side, precision=lax.Precision.HIGHEST)

def layer_norm(values, gain_row, shift_row):
    center = values - lax.optimization_barrier(jnp.mean(values, -1, keepdims=True))
    variance = lax.optimization_barrier(jnp.mean(center * center, -1, keepdims=True))
    return center * lax.rsqrt(variance + LN_EPS) * gain_row + shift_row

def forward(inputs, master_qkv, master_proj, master_fc1, master_fc2, master_vectors):
    w_qkv = low(master_qkv)
    w_proj = low(master_proj)
    w_fc1 = low(master_fc1)
    w_fc2 = low(master_fc2)
    vectors = low(master_vectors)
    slot_count = inputs.shape[0]
    length = inputs.shape[1]
    feature_width = inputs.shape[2]
    head_shape = (slot_count, length, HEADS, HEAD_DIM)
    fc1_bias = vectors[8:].reshape(-1)
    normed_one = low(layer_norm(inputs, vectors[0], vectors[1]))
    joined = product(normed_one, w_qkv)
    queries = low(low_back(joined[..., :feature_width] + vectors[2])).reshape(head_shape)
    keys_all = low(low_back(joined[..., feature_width:2 * feature_width])).reshape(head_shape)
    values_all = low(low_back(joined[..., 2 * feature_width:] + vectors[3])).reshape(head_shape)
    scores = jnp.einsum('bqhd,bkhd->bhqk', queries, keys_all, precision=lax.Precision.HIGHEST) * HEAD_DIM ** (-0.5)
    scores = low_back(scores)
    probs = low(jax.nn.softmax(scores, axis=-1))
    attended = jnp.einsum('bhqk,bkhd->bqhd', probs, values_all, precision=lax.Precision.HIGHEST)
    attended = low(low_back(attended.reshape(slot_count, length, feature_width)))
    mixed_rows = inputs + low_back(product(attended, w_proj) + vectors[4])
    normed_two = low(layer_norm(mixed_rows, vectors[5], vectors[6]))
    pre_act = low_back(product(normed_two, w_fc1) + fc1_bias)
    activated = low(jax.nn.gelu(pre_act, approximate=False))
    return mixed_rows + low_back(product(activated, w_fc2) + vectors[7])

def adamw(gradient, first_old, second_old, master, step_rate, decay_rate):
    first_new = BETA_ONE * first_old + (1.0 - BETA_ONE) * gradient
    second_new = BETA_TWO * second_old + (1.0 - BETA_TWO) * gradient * gradient
    first_hat = first_new / (1.0 - BETA_ONE ** STEP)
    second_hat = second_new / (1.0 - BETA_TWO ** STEP)
    master_new = master - step_rate * (first_hat / (jnp.sqrt(second_hat) + ADAM_EPS) + decay_rate * master)
    return (master_new, first_new, second_new)

def reference(images, cotangent, counts, master_qkv, master_proj, master_fc1, master_fc2, master_vectors, first_qkv, first_proj, first_fc1, first_fc2, first_vectors, second_qkv, second_proj, second_fc1, second_fc2, second_vectors):
    masters = (master_qkv, master_proj, master_fc1, master_fc2, master_vectors)
    image_groups = images.astype(jnp.float32).reshape(GROUPS, CAP, SEQ, D)
    cot_groups = cotangent.astype(jnp.float32).reshape(GROUPS, CAP, SEQ, D)
    slot_index = jnp.arange(CAP, dtype=jnp.int32)
    live_groups = (slot_index[None, :] < counts[:, None]).astype(jnp.float32)

    def device_step(totals, pieces):
        image_one, cot_one, live_one = pieces
        result, pullback = jax.vjp(forward, image_one, master_qkv, master_proj, master_fc1, master_fc2, master_vectors)
        slot_mask = live_one[:, None, None]
        grads = pullback(cot_one * slot_mask)
        totals = tuple((total + grad_one for total, grad_one in zip(totals, grads[1:])))
        return (totals, ((result * slot_mask).astype(jnp.bfloat16), grads[0]))
    start_totals = tuple((jnp.zeros_like(master) for master in masters))
    sums, stacked = lax.scan(device_step, start_totals, (image_groups, cot_groups, live_groups))
    block_out = stacked[0].reshape(SLOTS_ALL, SEQ, D)
    grad_input = stacked[1].reshape(SLOTS_ALL, SEQ, D)
    grad_qkv, grad_proj, grad_fc1, grad_fc2, grad_vectors = sums
    new_qkv = adamw(grad_qkv, first_qkv, second_qkv, master_qkv, RATE_MATRIX, DECAY_MATRIX)
    new_proj = adamw(grad_proj, first_proj, second_proj, master_proj, RATE_MATRIX, DECAY_MATRIX)
    new_fc1 = adamw(grad_fc1, first_fc1, second_fc1, master_fc1, RATE_MATRIX, DECAY_MATRIX)
    new_fc2 = adamw(grad_fc2, first_fc2, second_fc2, master_fc2, RATE_MATRIX, DECAY_MATRIX)
    new_vectors = adamw(grad_vectors, first_vectors, second_vectors, master_vectors, RATE_VECTOR, 0.0)
    return (block_out, grad_input, grad_qkv, grad_proj, grad_fc1, grad_fc2, grad_vectors, new_qkv[0], new_proj[0], new_fc1[0], new_fc2[0], new_vectors[0], new_qkv[1], new_proj[1], new_fc1[1], new_fc2[1], new_vectors[1], new_qkv[2], new_proj[2], new_fc1[2], new_fc2[2], new_vectors[2])
```

```python
from functools import partial

import jax
import jax.numpy as jnp
from jax import lax
from jax.experimental import pallas as pl
from jax.experimental.pallas import tpu as pltpu
from jax.sharding import PartitionSpec as P

HEADS = 12
STEP = 10


LN_EPS = 1e-06
BETA_ONE = 0.9
BETA_TWO = 0.999
ADAM_EPS = 1e-08
RATE_MATRIX = 0.05
RATE_VECTOR = 0.2
DECAY_MATRIX = 0.05


def layer_stats(values):
    center = values - jnp.mean(values, -1, keepdims=True)
    inverse = lax.rsqrt(jnp.mean(center * center, -1, keepdims=True) + LN_EPS)
    return (center * inverse, inverse)


def norm_back(grad_rows, normed, inverse, gain_row):
    scaled = grad_rows * gain_row
    return inverse * (
        scaled
        - jnp.mean(scaled, -1, keepdims=True)
        - normed * jnp.mean(scaled * normed, -1, keepdims=True)
    )


def left_product(left_side, right_side):
    return lax.dot_general(
        left_side, right_side, (((0,), (0,)), ((), ())), preferred_element_type=jnp.float32
    )


def right_product(left_side, right_side):
    return lax.dot_general(
        left_side, right_side, (((1,), (1,)), ((), ())), preferred_element_type=jnp.float32
    )


def adamw(gradient, first_old, second_old, master, step_rate, decay_rate):
    first_new = BETA_ONE * first_old + (1.0 - BETA_ONE) * gradient
    second_new = BETA_TWO * second_old + (1.0 - BETA_TWO) * gradient * gradient
    first_hat = first_new / (1.0 - BETA_ONE**STEP)
    second_hat = second_new / (1.0 - BETA_TWO**STEP)
    master_new = master - step_rate * (
        first_hat / (jnp.sqrt(second_hat) + ADAM_EPS) + decay_rate * master
    )
    return (master_new, first_new, second_new)


def swap(value, axis, size, bit):
    return lax.ppermute(value, axis, [(i, i ^ (1 << bit)) for i in range(size)])


def bit_orders(size):
    chip_bits = list(range(1, size.bit_length() - 1))
    half = len(chip_bits) // 2
    return chip_bits, chip_bits[half:] + chip_bits[:half]


def gather_bits(value, held_bits, order, size):
    index = lax.axis_index("zero")
    held_bits = list(held_bits)
    for bit in order:
        other = swap(value, "zero", size, bit)
        first = (index >> bit) & 1 == 0
        place = sum(1 for held in held_bits if held > bit)
        value = jnp.stack(
            [jnp.where(first, value, other), jnp.where(first, other, value)], axis=place
        )
        held_bits.append(bit)
    return value, held_bits


def gather_rows(block):
    size = lax.axis_size("zero")
    rows, columns = block.shape
    low = block.astype(jnp.bfloat16)
    order_one, order_two = bit_orders(size)
    part_one, held = gather_bits(low[: rows // 2], [], order_one[::-1], size)
    part_two, _ = gather_bits(low[rows // 2 :], [], order_two[::-1], size)
    whole = jnp.concatenate([part_one, part_two], axis=-2)
    whole, _ = gather_bits(whole, held, [0], size)
    return whole.reshape(size * rows, columns)


def halve_bits(value, held_bits, order, size):
    index = lax.axis_index("zero")
    held_bits = list(held_bits)
    for bit in order:
        place = held_bits.index(bit)
        mine = (index >> bit) & 1
        sent = lax.dynamic_index_in_dim(value, 1 - mine, place, keepdims=False)
        kept = lax.dynamic_index_in_dim(value, mine, place, keepdims=False)
        came = swap(sent, "zero", size, bit)
        value = (kept.astype(jnp.float32) + came.astype(jnp.float32)).astype(value.dtype)
        held_bits.remove(bit)
    return value, held_bits


def sum_line(value):
    count = lax.axis_size("dp")
    if count % 2 == 1:
        return lax.psum(value.astype(jnp.float32), "dp")
    index = lax.axis_index("dp")
    half = count // 2

    def add(left, right):
        return (left.astype(jnp.float32) + right.astype(jnp.float32)).astype(value.dtype)

    total = value
    for step in range(half - 1):
        pairs = [(step, step + 1), (count - 1 - step, count - 2 - step)]
        total = add(total, lax.ppermute(total, "dp", pairs))
    total = add(total, lax.ppermute(total, "dp", [(half - 1, half), (half, half - 1)]))
    for step in range(half - 2, -1, -1):
        pairs = [(step + 1, step), (count - 2 - step, count - 1 - step)]
        came = lax.ppermute(total, "dp", pairs)
        total = jnp.where((index == step) | (index == count - 1 - step), came, total)
    return total.astype(jnp.float32)


def reduce_rows(partial_sum):
    size = lax.axis_size("zero")
    rows = partial_sum.shape[0] // size
    columns = partial_sum.shape[1]
    bits = size.bit_length() - 1
    held = list(range(bits - 1, -1, -1))
    order_one, order_two = bit_orders(size)
    value = partial_sum.reshape((2,) * bits + (rows, columns))
    value, held = halve_bits(value, held, [0], size)
    part_one, _ = halve_bits(value[..., : rows // 2, :], held, order_one, size)
    part_two, _ = halve_bits(value[..., rows // 2 :, :], held, order_two, size)
    return jnp.concatenate([sum_line(part_one), sum_line(part_two)], axis=0)


def gather_vectors(block):
    size = lax.axis_size("zero")
    order_one, _ = bit_orders(size)
    whole, _ = gather_bits(block.astype(jnp.bfloat16), [], order_one[::-1] + [0], size)
    rows, columns = block.shape
    return whole.reshape(size, rows, columns).transpose(1, 0, 2).reshape(rows, size * columns)


def reduce_vectors(partial_sum):
    size = lax.axis_size("zero")
    rows, columns = partial_sum.shape
    bits = size.bit_length() - 1
    order_one, _ = bit_orders(size)
    value = partial_sum.reshape(rows, size, columns // size).transpose(1, 0, 2)
    value = value.reshape((2,) * bits + (rows, columns // size))
    value, _ = halve_bits(value, list(range(bits - 1, -1, -1)), [0] + order_one, size)
    return sum_line(value)


def contract(left_side, right_side, left_dim, right_dim):
    return lax.dot_general(
        left_side,
        right_side,
        (((left_dim,), (right_dim,)), ((), ())),
        preferred_element_type=jnp.float32,
    )


def head_masks(padded):
    lane = lax.broadcasted_iota(jnp.int32, (padded, 128), 1)
    return lane < 64, lane >= 64


def attend_kernel(length, scale, joined_ref, attn_ref, lse_ref):
    padded, width = attn_ref.shape[1:]
    masks = head_masks(padded)
    live = lax.broadcasted_iota(jnp.int32, (padded, padded), 0) < length
    zero = jnp.zeros((padded, 128), jnp.bfloat16)
    for pair in range(width // 128):
        at = pair * 128
        queries = joined_ref[0, :, at : at + 128] * jnp.bfloat16(scale)
        keys = joined_ref[0, :, width + at : width + at + 128]
        values = joined_ref[0, :, 2 * width + at : 2 * width + at + 128]
        outs = []
        for half in range(2):
            query = jnp.where(masks[half], queries, zero)
            scores = jnp.where(live, contract(keys, query, 1, 1), -1e30)
            highest = jnp.max(scores, 0, keepdims=True)
            exponent = jnp.exp(scores - highest)
            total = jnp.sum(exponent, 0, keepdims=True)
            head = 2 * pair + half
            lse_ref[0, head : head + 1, :] = highest + jnp.log(total)
            probs = (exponent * (1.0 / total)).astype(jnp.bfloat16)
            outs.append(contract(probs, values, 0, 0))
        attn_ref[0, :, at : at + 128] = jnp.where(masks[0], outs[0], outs[1]).astype(jnp.bfloat16)


def attend_back_kernel(length, scale, joined_ref, lse_ref, back_ref, out_ref):
    padded, width = back_ref.shape[1:]
    masks = head_masks(padded)
    live = lax.broadcasted_iota(jnp.int32, (padded, padded), 0) < length
    zero = jnp.zeros((padded, 128), jnp.bfloat16)
    for pair in range(width // 128):
        at = pair * 128
        queries = joined_ref[0, :, at : at + 128] * jnp.bfloat16(scale)
        keys = joined_ref[0, :, width + at : width + at + 128]
        keys_scaled = keys * jnp.bfloat16(scale)
        values = joined_ref[0, :, 2 * width + at : 2 * width + at + 128]
        backs = back_ref[0, :, at : at + 128]
        grads = [0.0, 0.0, 0.0]
        for half in range(2):
            head = 2 * pair + half
            query = jnp.where(masks[half], queries, zero)
            key = jnp.where(masks[half], keys_scaled, zero)
            back = jnp.where(masks[half], backs, zero)
            scores = contract(keys, query, 1, 1)
            probs = jnp.where(live, jnp.exp(scores - lse_ref[0, head : head + 1, :]), 0.0)
            grad_probs = contract(values, back, 1, 1)
            inner = jnp.sum(probs * grad_probs, 0, keepdims=True)
            low = (probs * (grad_probs - inner)).astype(jnp.bfloat16)
            grads[0] += contract(low, key, 0, 0)
            grads[1] += contract(low, query, 1, 0)
            grads[2] += contract(probs.astype(jnp.bfloat16), back, 1, 0)
        for part in range(3):
            start = part * width + at
            out_ref[0, :, start : start + 128] = grads[part].astype(jnp.bfloat16)


def slot_block(rows, columns):
    return pl.BlockSpec((1, rows, columns), lambda slot: (slot, 0, 0))


KERNEL_PARAMS = pltpu.CompilerParams(vmem_limit_bytes=40 * 2**20)


def attend(joined, length, scale, head_rows):
    slots, padded, triple = joined.shape
    width = triple // 3
    return pl.pallas_call(
        partial(attend_kernel, length, scale),
        grid=(slots,),
        in_specs=[slot_block(padded, triple)],
        out_specs=[slot_block(padded, width), slot_block(head_rows, padded)],
        out_shape=[
            jax.ShapeDtypeStruct((slots, padded, width), jnp.bfloat16),
            jax.ShapeDtypeStruct((slots, head_rows, padded), jnp.float32),
        ],
        compiler_params=KERNEL_PARAMS,
        cost_estimate=pl.CostEstimate(
            flops=slots * 12 * padded * padded * 64 * 16,
            bytes_accessed=slots * padded * width * 8,
            transcendentals=slots * 12 * padded * padded,
        ),
        name="attend",
    )(joined)


def attend_back(joined, lse, back, length, scale):
    slots, padded, triple = joined.shape
    width = triple // 3
    return pl.pallas_call(
        partial(attend_back_kernel, length, scale),
        grid=(slots,),
        in_specs=[
            slot_block(padded, triple),
            slot_block(lse.shape[1], padded),
            slot_block(padded, width),
        ],
        out_specs=slot_block(padded, triple),
        out_shape=jax.ShapeDtypeStruct((slots, padded, triple), jnp.bfloat16),
        compiler_params=KERNEL_PARAMS,
        cost_estimate=pl.CostEstimate(
            flops=slots * 12 * padded * padded * 64 * 40,
            bytes_accessed=slots * padded * width * 14,
            transcendentals=slots * 12 * padded * padded,
        ),
        name="attend_back",
    )(joined, lse, back)


def per_device(
    images,
    cotangent,
    counts,
    master_qkv,
    master_proj,
    master_fc1,
    master_fc2,
    master_vectors,
    first_qkv,
    first_proj,
    first_fc1,
    first_fc2,
    first_vectors,
    second_qkv,
    second_proj,
    second_fc1,
    second_fc2,
    second_vectors,
):
    vectors = gather_vectors(master_vectors).astype(jnp.float32)
    w_qkv = gather_rows(master_qkv)
    w_proj = gather_rows(master_proj)
    w_fc1 = gather_rows(master_fc1)
    w_fc2 = gather_rows(master_fc2)
    slot_count, length, feature_width = images.shape
    padded = -(-length // 16) * 16
    row_count = slot_count * padded
    head_width = feature_width // HEADS
    score_scale = head_width ** (-0.5)
    slot_shape = (slot_count, padded, feature_width)
    slot_live = (lax.iota(jnp.int32, slot_count) < counts[0]).astype(jnp.float32)
    row_live = jnp.repeat(slot_live, padded)[:, None]
    more_rows = ((0, 0), (0, padded - length), (0, 0))
    inputs = (
        jnp.pad(images, more_rows).astype(jnp.float32).reshape(row_count, feature_width)
    )
    normed_one, inverse_one = layer_stats(inputs)
    hidden_one = (normed_one * vectors[0] + vectors[1]).astype(jnp.bfloat16)
    joined_bias = jnp.concatenate([vectors[2], jnp.zeros_like(vectors[2]), vectors[3]])
    joined = (
        (jnp.dot(hidden_one, w_qkv, preferred_element_type=jnp.float32) + joined_bias)
        .astype(jnp.bfloat16)
        .reshape(slot_count, padded, 3 * feature_width)
    )
    attn_slots, log_total = attend(joined, length, score_scale, 16)
    attn_low = attn_slots.reshape(row_count, feature_width)
    mixed_rows = inputs + jnp.dot(attn_low, w_proj, preferred_element_type=jnp.float32) + vectors[4]
    normed_two, inverse_two = layer_stats(mixed_rows)
    hidden_two = (normed_two * vectors[5] + vectors[6]).astype(jnp.bfloat16)
    fc1_bias = vectors[8:].reshape(-1)
    pre_act = jnp.dot(hidden_two, w_fc1, preferred_element_type=jnp.float32) + fc1_bias
    act_value, gelu_back = jax.vjp(partial(jax.nn.gelu, approximate=False), pre_act)
    act_low = act_value.astype(jnp.bfloat16)
    block_rows = (
        mixed_rows + jnp.dot(act_low, w_fc2, preferred_element_type=jnp.float32) + vectors[7]
    )
    block_out = (block_rows * row_live).astype(jnp.bfloat16).reshape(slot_shape)[:, :length]
    grad_rows = (
        jnp.pad(cotangent, more_rows).astype(jnp.float32).reshape(row_count, feature_width)
        * row_live
    )
    grad_low = grad_rows.astype(jnp.bfloat16)
    sum_fc2 = reduce_rows(left_product(act_low, grad_low).astype(jnp.bfloat16))
    bias_fc2 = jnp.sum(grad_low.astype(jnp.float32), 0)
    grad_pre = gelu_back(right_product(grad_low, w_fc2))[0]
    pre_low = grad_pre.astype(jnp.bfloat16)
    sum_fc1 = reduce_rows(left_product(hidden_two, pre_low).astype(jnp.bfloat16))
    bias_fc1 = jnp.sum(pre_low.astype(jnp.float32), 0)
    back_two = right_product(pre_low, w_fc1)
    gain_two = jnp.sum(back_two * normed_two, 0)
    shift_two = jnp.sum(back_two, 0)
    grad_mixed = grad_rows + norm_back(back_two, normed_two, inverse_two, vectors[5])
    mixed_low = grad_mixed.astype(jnp.bfloat16)
    sum_proj = reduce_rows(left_product(attn_low, mixed_low).astype(jnp.bfloat16))
    bias_proj = jnp.sum(mixed_low.astype(jnp.float32), 0)
    back_attn = right_product(mixed_low, w_proj).astype(jnp.bfloat16).reshape(slot_shape)
    grad_joined = attend_back(joined, log_total, back_attn, length, score_scale).reshape(
        row_count, 3 * feature_width
    )
    sum_qkv = reduce_rows(left_product(hidden_one, grad_joined).astype(jnp.bfloat16))
    bias_query = jnp.sum(grad_joined[:, :feature_width].astype(jnp.float32), 0)
    bias_value = jnp.sum(grad_joined[:, 2 * feature_width :].astype(jnp.float32), 0)
    back_one = right_product(grad_joined, w_qkv)
    gain_one = jnp.sum(back_one * normed_one, 0)
    shift_one = jnp.sum(back_one, 0)
    grad_input = (
        grad_mixed + norm_back(back_one, normed_one, inverse_one, vectors[0])
    ).reshape(slot_shape)[:, :length]
    grad_vectors = jnp.concatenate(
        [
            jnp.stack(
                [
                    gain_one,
                    shift_one,
                    bias_query,
                    bias_value,
                    bias_proj,
                    gain_two,
                    shift_two,
                    bias_fc2,
                ]
            ),
            bias_fc1.reshape(-1, feature_width),
        ],
        0,
    )
    sum_vectors = reduce_vectors(grad_vectors)
    new_qkv = adamw(sum_qkv, first_qkv, second_qkv, master_qkv, RATE_MATRIX, DECAY_MATRIX)
    new_proj = adamw(sum_proj, first_proj, second_proj, master_proj, RATE_MATRIX, DECAY_MATRIX)
    new_fc1 = adamw(sum_fc1, first_fc1, second_fc1, master_fc1, RATE_MATRIX, DECAY_MATRIX)
    new_fc2 = adamw(sum_fc2, first_fc2, second_fc2, master_fc2, RATE_MATRIX, DECAY_MATRIX)
    new_vectors = adamw(
        sum_vectors, first_vectors, second_vectors, master_vectors, RATE_VECTOR, 0.0
    )
    return (
        block_out,
        grad_input,
        sum_qkv,
        sum_proj,
        sum_fc1,
        sum_fc2,
        sum_vectors,
        new_qkv[0],
        new_proj[0],
        new_fc1[0],
        new_fc2[0],
        new_vectors[0],
        new_qkv[1],
        new_proj[1],
        new_fc1[1],
        new_fc2[1],
        new_vectors[1],
        new_qkv[2],
        new_proj[2],
        new_fc1[2],
        new_fc2[2],
        new_vectors[2],
    )


def solution(mesh):
    placed = (
        P(("dp", "zero"), None, None),
        P(("dp", "zero"), None, None),
        P(("dp", "zero")),
        P("zero", None),
        P("zero", None),
        P("zero", None),
        P("zero", None),
        P(None, "zero"),
        P("zero", None),
        P("zero", None),
        P("zero", None),
        P("zero", None),
        P(None, "zero"),
        P("zero", None),
        P("zero", None),
        P("zero", None),
        P("zero", None),
        P(None, "zero"),
    )
    return jax.shard_map(
        per_device,
        mesh=mesh,
        in_specs=placed,
        out_specs=(
            P(("dp", "zero"), None, None),
            P(("dp", "zero"), None, None),
            P("zero", None),
            P("zero", None),
            P("zero", None),
            P("zero", None),
            P(None, "zero"),
            P("zero", None),
            P("zero", None),
            P("zero", None),
            P("zero", None),
            P(None, "zero"),
            P("zero", None),
            P("zero", None),
            P("zero", None),
            P("zero", None),
            P(None, "zero"),
            P("zero", None),
            P("zero", None),
            P("zero", None),
            P("zero", None),
            P(None, "zero"),
        ),
        check_vma=False,
    )
```

```python
from functools import partial

import jax
import jax.numpy as jnp
from jax import lax
from jax.experimental import pallas as pl
from jax.experimental.pallas import tpu as pltpu
from jax.sharding import PartitionSpec as P

HEADS = 12
STEP = 10


LN_EPS = 1e-06
BETA_ONE = 0.9
BETA_TWO = 0.999
ADAM_EPS = 1e-08
RATE_MATRIX = 0.05
RATE_VECTOR = 0.2
DECAY_MATRIX = 0.05


def layer_stats(values):
    center = values - jnp.mean(values, -1, keepdims=True)
    inverse = lax.rsqrt(jnp.mean(center * center, -1, keepdims=True) + LN_EPS)
    return (center * inverse, inverse)


def norm_back(grad_rows, normed, inverse, gain_row):
    scaled = grad_rows * gain_row
    return inverse * (
        scaled
        - jnp.mean(scaled, -1, keepdims=True)
        - normed * jnp.mean(scaled * normed, -1, keepdims=True)
    )


def left_product(left_side, right_side):
    return lax.dot_general(
        left_side, right_side, (((0,), (0,)), ((), ())), preferred_element_type=jnp.float32
    )


def right_product(left_side, right_side):
    return lax.dot_general(
        left_side, right_side, (((1,), (1,)), ((), ())), preferred_element_type=jnp.float32
    )


def adamw(gradient, first_old, second_old, master, step_rate, decay_rate):
    first_new = BETA_ONE * first_old + (1.0 - BETA_ONE) * gradient
    second_new = BETA_TWO * second_old + (1.0 - BETA_TWO) * gradient * gradient
    first_hat = first_new / (1.0 - BETA_ONE**STEP)
    second_hat = second_new / (1.0 - BETA_TWO**STEP)
    master_new = master - step_rate * (
        first_hat / (jnp.sqrt(second_hat) + ADAM_EPS) + decay_rate * master
    )
    return (master_new, first_new, second_new)


def swap(value, axis, size, bit):
    return lax.ppermute(value, axis, [(i, i ^ (1 << bit)) for i in range(size)])


def bit_orders(size):
    chip_bits = list(range(1, size.bit_length() - 1))
    half = len(chip_bits) // 2
    return chip_bits, chip_bits[half:] + chip_bits[:half]


def gather_bits(value, held_bits, order, size):
    index = lax.axis_index("zero")
    held_bits = list(held_bits)
    for bit in order:
        other = swap(value, "zero", size, bit)
        first = (index >> bit) & 1 == 0
        place = sum(1 for held in held_bits if held > bit)
        value = jnp.stack(
            [jnp.where(first, value, other), jnp.where(first, other, value)], axis=place
        )
        held_bits.append(bit)
    return value, held_bits


class Pipe:
    def __init__(self, stages):
        self.stages = stages
        self.state = next(stages)
        self.done = False

    def advance(self):
        try:
            self.state = self.stages.send(self.state)
        except StopIteration as end:
            self.state, self.done = end.value, True


def tick(pipes, values):
    active = [pipe for pipe in pipes if not pipe.done]
    for pipe in active:
        pipe.advance()
    values, states = lax.optimization_barrier((values, [pipe.state for pipe in active]))
    for pipe, state in zip(active, states):
        pipe.state = state
    return values


def drain(pipes, values):
    while not all(pipe.done for pipe in pipes):
        values = tick(pipes, values)
    return values


def gather_rows(block):
    size = lax.axis_size("zero")
    rows, columns = block.shape
    low = block.astype(jnp.bfloat16)
    order_one, order_two = bit_orders(size)
    parts = yield (low[: rows // 2], low[rows // 2 :])
    held_one, held_two = [], []
    for bit_one, bit_two in zip(order_one[::-1], order_two[::-1]):
        part_one, held_one = gather_bits(parts[0], held_one, [bit_one], size)
        part_two, held_two = gather_bits(parts[1], held_two, [bit_two], size)
        parts = yield (part_one, part_two)
    whole = jnp.concatenate(parts, axis=-2)
    whole, _ = gather_bits(whole, held_one, [0], size)
    return whole.reshape(size * rows, columns)


def halve_bits(value, held_bits, order, size):
    index = lax.axis_index("zero")
    held_bits = list(held_bits)
    for bit in order:
        place = held_bits.index(bit)
        mine = (index >> bit) & 1
        sent = lax.dynamic_index_in_dim(value, 1 - mine, place, keepdims=False)
        kept = lax.dynamic_index_in_dim(value, mine, place, keepdims=False)
        came = swap(sent, "zero", size, bit)
        value = (kept.astype(jnp.float32) + came.astype(jnp.float32)).astype(value.dtype)
        held_bits.remove(bit)
    return value, held_bits


def sum_line(values):
    count = lax.axis_size("dp")
    if count % 2 == 1:
        return [lax.psum(value.astype(jnp.float32), "dp") for value in values]
    index = lax.axis_index("dp")
    half = count // 2

    def add(left, right):
        return (left.astype(jnp.float32) + right.astype(jnp.float32)).astype(left.dtype)

    for step in range(half - 1):
        pairs = [(step, step + 1), (count - 1 - step, count - 2 - step)]
        values = yield [add(value, lax.ppermute(value, "dp", pairs)) for value in values]
    pairs = [(half - 1, half), (half, half - 1)]
    values = yield [add(value, lax.ppermute(value, "dp", pairs)) for value in values]
    for step in range(half - 2, -1, -1):
        pairs = [(step + 1, step), (count - 2 - step, count - 1 - step)]
        outer = (index == step) | (index == count - 1 - step)
        values = yield [
            jnp.where(outer, lax.ppermute(value, "dp", pairs), value) for value in values
        ]
    return [value.astype(jnp.float32) for value in values]


def reduce_rows(partial_sum):
    size = lax.axis_size("zero")
    rows = partial_sum.shape[0] // size
    columns = partial_sum.shape[1]
    bits = size.bit_length() - 1
    held = list(range(bits - 1, -1, -1))
    order_one, order_two = bit_orders(size)
    value = yield partial_sum.reshape((2,) * bits + (rows, columns))
    value, held = halve_bits(value, held, [0], size)
    value = yield value
    parts = (value[..., : rows // 2, :], value[..., rows // 2 :, :])
    held_one, held_two = held, held
    for bit_one, bit_two in zip(order_one, order_two):
        part_one, held_one = halve_bits(parts[0], held_one, [bit_one], size)
        part_two, held_two = halve_bits(parts[1], held_two, [bit_two], size)
        parts = yield (part_one, part_two)
    parts = yield from sum_line(list(parts))
    return jnp.concatenate(parts, axis=0)


def gather_vectors(block):
    size = lax.axis_size("zero")
    order_one, _ = bit_orders(size)
    whole = yield block.astype(jnp.bfloat16)
    held = []
    for bit in order_one[::-1]:
        whole, held = gather_bits(whole, held, [bit], size)
        whole = yield whole
    whole, held = gather_bits(whole, held, [0], size)
    rows, columns = block.shape
    return whole.reshape(size, rows, columns).transpose(1, 0, 2).reshape(rows, size * columns)


def reduce_vectors(partial_sum):
    size = lax.axis_size("zero")
    rows, columns = partial_sum.shape
    bits = size.bit_length() - 1
    order_one, _ = bit_orders(size)
    value = partial_sum.reshape(rows, size, columns // size).transpose(1, 0, 2)
    value = yield value.reshape((2,) * bits + (rows, columns // size))
    held = list(range(bits - 1, -1, -1))
    for bit in [0] + order_one:
        value, held = halve_bits(value, held, [bit], size)
        value = yield value
    (value,) = yield from sum_line([value])
    return value


def contract(left_side, right_side, left_dim, right_dim):
    return lax.dot_general(
        left_side,
        right_side,
        (((left_dim,), (right_dim,)), ((), ())),
        preferred_element_type=jnp.float32,
    )


def head_masks(padded):
    lane = lax.broadcasted_iota(jnp.int32, (padded, 128), 1)
    return lane < 64, lane >= 64


def attend_kernel(length, scale, joined_ref, attn_ref, lse_ref):
    padded, width = attn_ref.shape[1:]
    masks = head_masks(padded)
    live = lax.broadcasted_iota(jnp.int32, (padded, padded), 0) < length
    zero = jnp.zeros((padded, 128), jnp.bfloat16)
    for pair in range(width // 128):
        at = pair * 128
        queries = joined_ref[0, :, at : at + 128] * jnp.bfloat16(scale)
        keys = joined_ref[0, :, width + at : width + at + 128]
        values = joined_ref[0, :, 2 * width + at : 2 * width + at + 128]
        outs = []
        for half in range(2):
            query = jnp.where(masks[half], queries, zero)
            scores = jnp.where(live, contract(keys, query, 1, 1), -1e30)
            highest = jnp.max(scores, 0, keepdims=True)
            exponent = jnp.exp(scores - highest)
            total = jnp.sum(exponent, 0, keepdims=True)
            head = 2 * pair + half
            lse_ref[0, head : head + 1, :] = highest + jnp.log(total)
            probs = (exponent * (1.0 / total)).astype(jnp.bfloat16)
            outs.append(contract(probs, values, 0, 0))
        attn_ref[0, :, at : at + 128] = jnp.where(masks[0], outs[0], outs[1]).astype(jnp.bfloat16)


def attend_back_kernel(length, scale, joined_ref, lse_ref, back_ref, out_ref):
    padded, width = back_ref.shape[1:]
    masks = head_masks(padded)
    live = lax.broadcasted_iota(jnp.int32, (padded, padded), 0) < length
    zero = jnp.zeros((padded, 128), jnp.bfloat16)
    for pair in range(width // 128):
        at = pair * 128
        queries = joined_ref[0, :, at : at + 128] * jnp.bfloat16(scale)
        keys = joined_ref[0, :, width + at : width + at + 128]
        keys_scaled = keys * jnp.bfloat16(scale)
        values = joined_ref[0, :, 2 * width + at : 2 * width + at + 128]
        backs = back_ref[0, :, at : at + 128]
        grads = [0.0, 0.0, 0.0]
        for half in range(2):
            head = 2 * pair + half
            query = jnp.where(masks[half], queries, zero)
            key = jnp.where(masks[half], keys_scaled, zero)
            back = jnp.where(masks[half], backs, zero)
            scores = contract(keys, query, 1, 1)
            probs = jnp.where(live, jnp.exp(scores - lse_ref[0, head : head + 1, :]), 0.0)
            grad_probs = contract(values, back, 1, 1)
            inner = jnp.sum(probs * grad_probs, 0, keepdims=True)
            low = (probs * (grad_probs - inner)).astype(jnp.bfloat16)
            grads[0] += contract(low, key, 0, 0)
            grads[1] += contract(low, query, 1, 0)
            grads[2] += contract(probs.astype(jnp.bfloat16), back, 1, 0)
        for part in range(3):
            start = part * width + at
            out_ref[0, :, start : start + 128] = grads[part].astype(jnp.bfloat16)


def slot_block(rows, columns):
    return pl.BlockSpec((1, rows, columns), lambda slot: (slot, 0, 0))


KERNEL_PARAMS = pltpu.CompilerParams(vmem_limit_bytes=40 * 2**20)


def attend(joined, length, scale, head_rows):
    slots, padded, triple = joined.shape
    width = triple // 3
    return pl.pallas_call(
        partial(attend_kernel, length, scale),
        grid=(slots,),
        in_specs=[slot_block(padded, triple)],
        out_specs=[slot_block(padded, width), slot_block(head_rows, padded)],
        out_shape=[
            jax.ShapeDtypeStruct((slots, padded, width), jnp.bfloat16),
            jax.ShapeDtypeStruct((slots, head_rows, padded), jnp.float32),
        ],
        compiler_params=KERNEL_PARAMS,
        cost_estimate=pl.CostEstimate(
            flops=slots * 12 * padded * padded * 64 * 16,
            bytes_accessed=slots * padded * width * 8,
            transcendentals=slots * 12 * padded * padded,
        ),
        name="attend",
    )(joined)


def attend_back(joined, lse, back, length, scale):
    slots, padded, triple = joined.shape
    width = triple // 3
    return pl.pallas_call(
        partial(attend_back_kernel, length, scale),
        grid=(slots,),
        in_specs=[
            slot_block(padded, triple),
            slot_block(lse.shape[1], padded),
            slot_block(padded, width),
        ],
        out_specs=slot_block(padded, triple),
        out_shape=jax.ShapeDtypeStruct((slots, padded, triple), jnp.bfloat16),
        compiler_params=KERNEL_PARAMS,
        cost_estimate=pl.CostEstimate(
            flops=slots * 12 * padded * padded * 64 * 40,
            bytes_accessed=slots * padded * width * 14,
            transcendentals=slots * 12 * padded * padded,
        ),
        name="attend_back",
    )(joined, lse, back)


def per_device(
    images,
    cotangent,
    counts,
    master_qkv,
    master_proj,
    master_fc1,
    master_fc2,
    master_vectors,
    first_qkv,
    first_proj,
    first_fc1,
    first_fc2,
    first_vectors,
    second_qkv,
    second_proj,
    second_fc1,
    second_fc2,
    second_vectors,
):
    get_vectors = Pipe(gather_vectors(master_vectors))
    get_qkv = Pipe(gather_rows(master_qkv))
    get_proj = Pipe(gather_rows(master_proj))
    get_fc1 = Pipe(gather_rows(master_fc1))
    get_fc2 = Pipe(gather_rows(master_fc2))
    slot_count, length, feature_width = images.shape
    padded = -(-length // 16) * 16
    row_count = slot_count * padded
    head_width = feature_width // HEADS
    score_scale = head_width ** (-0.5)
    slot_shape = (slot_count, padded, feature_width)
    slot_live = (lax.iota(jnp.int32, slot_count) < counts[0]).astype(jnp.float32)
    row_live = jnp.repeat(slot_live, padded)[:, None]
    more_rows = ((0, 0), (0, padded - length), (0, 0))
    inputs = (
        jnp.pad(images, more_rows).astype(jnp.float32).reshape(row_count, feature_width)
    )
    normed_one, inverse_one = layer_stats(inputs)
    tick([get_qkv, get_vectors], ())
    normed_one, inverse_one = tick(
        [get_qkv, get_vectors, get_proj], (normed_one, inverse_one)
    )
    while not get_qkv.done:
        tick([get_qkv, get_vectors, get_proj, get_fc1], ())
    w_qkv = get_qkv.state
    vectors = get_vectors.state.astype(jnp.float32)
    hidden_one = (normed_one * vectors[0] + vectors[1]).astype(jnp.bfloat16)
    joined_bias = jnp.concatenate([vectors[2], jnp.zeros_like(vectors[2]), vectors[3]])
    joined = (
        (jnp.dot(hidden_one, w_qkv, preferred_element_type=jnp.float32) + joined_bias)
        .astype(jnp.bfloat16)
        .reshape(slot_count, padded, 3 * feature_width)
    )
    attn_slots, log_total = attend(joined, length, score_scale, 16)
    attn_slots, log_total = tick([get_proj, get_fc1, get_fc2], (attn_slots, log_total))
    drain([get_proj], ())
    w_proj = get_proj.state
    attn_low = attn_slots.reshape(row_count, feature_width)
    mixed_rows = inputs + jnp.dot(attn_low, w_proj, preferred_element_type=jnp.float32) + vectors[4]
    normed_two, inverse_two = layer_stats(mixed_rows)
    hidden_two = (normed_two * vectors[5] + vectors[6]).astype(jnp.bfloat16)
    hidden_two = drain([get_fc1], hidden_two)
    w_fc1 = get_fc1.state
    fc1_bias = vectors[8:].reshape(-1)
    pre_act = jnp.dot(hidden_two, w_fc1, preferred_element_type=jnp.float32) + fc1_bias
    act_value, gelu_back = jax.vjp(partial(jax.nn.gelu, approximate=False), pre_act)
    act_low = act_value.astype(jnp.bfloat16)
    while not get_fc2.done:
        get_fc2.advance()
    act_low, w_fc2 = lax.optimization_barrier((act_low, get_fc2.state))
    grad_rows = (
        jnp.pad(cotangent, more_rows).astype(jnp.float32).reshape(row_count, feature_width)
        * row_live
    )
    grad_low = grad_rows.astype(jnp.bfloat16)
    partial_fc2 = left_product(act_low, grad_low).astype(jnp.bfloat16)
    partial_fc2, grad_low = lax.optimization_barrier((partial_fc2, grad_low))
    put_fc2 = Pipe(reduce_rows(partial_fc2))
    bias_fc2 = jnp.sum(grad_low.astype(jnp.float32), 0)
    grad_pre = gelu_back(right_product(grad_low, w_fc2))[0]
    pre_low = tick([put_fc2], grad_pre.astype(jnp.bfloat16))
    partial_fc1 = left_product(hidden_two, pre_low).astype(jnp.bfloat16)
    partial_fc1, pre_low = tick([put_fc2], (partial_fc1, pre_low))
    put_fc1 = Pipe(reduce_rows(partial_fc1))
    bias_fc1 = jnp.sum(pre_low.astype(jnp.float32), 0)
    back_two = right_product(pre_low, w_fc1)
    gain_two = jnp.sum(back_two * normed_two, 0)
    shift_two = jnp.sum(back_two, 0)
    grad_mixed = grad_rows + norm_back(back_two, normed_two, inverse_two, vectors[5])
    mixed_low = grad_mixed.astype(jnp.bfloat16)
    mixed_low = tick([put_fc2, put_fc1], mixed_low)
    partial_proj = left_product(attn_low, mixed_low).astype(jnp.bfloat16)
    bias_proj = jnp.sum(mixed_low.astype(jnp.float32), 0)
    back_attn = right_product(mixed_low, w_proj).astype(jnp.bfloat16).reshape(slot_shape)
    grad_joined = attend_back(joined, log_total, back_attn, length, score_scale).reshape(
        row_count, 3 * feature_width
    )
    partial_proj, grad_joined = tick([put_fc2, put_fc1], (partial_proj, grad_joined))
    put_proj = Pipe(reduce_rows(partial_proj))
    partial_qkv = left_product(hidden_one, grad_joined).astype(jnp.bfloat16)
    partial_qkv, grad_joined = tick([put_fc2, put_fc1, put_proj], (partial_qkv, grad_joined))
    put_qkv = Pipe(reduce_rows(partial_qkv))
    bias_query = jnp.sum(grad_joined[:, :feature_width].astype(jnp.float32), 0)
    bias_value = jnp.sum(grad_joined[:, 2 * feature_width :].astype(jnp.float32), 0)
    back_one = right_product(grad_joined, w_qkv)
    gain_one = jnp.sum(back_one * normed_one, 0)
    shift_one = jnp.sum(back_one, 0)
    grad_input = (
        grad_mixed + norm_back(back_one, normed_one, inverse_one, vectors[0])
    ).reshape(slot_shape)[:, :length]
    grad_vectors = jnp.concatenate(
        [
            jnp.stack(
                [
                    gain_one,
                    shift_one,
                    bias_query,
                    bias_value,
                    bias_proj,
                    gain_two,
                    shift_two,
                    bias_fc2,
                ]
            ),
            bias_fc1.reshape(-1, feature_width),
        ],
        0,
    )
    act_low, grad_vectors = tick(
        [put_fc2, put_fc1, put_proj, put_qkv], (act_low, grad_vectors)
    )
    put_vectors = Pipe(reduce_vectors(grad_vectors))
    block_rows = (
        mixed_rows + jnp.dot(act_low, w_fc2, preferred_element_type=jnp.float32) + vectors[7]
    )
    block_out = (block_rows * row_live).astype(jnp.bfloat16).reshape(slot_shape)[:, :length]
    drain([put_fc2, put_fc1, put_proj, put_qkv, put_vectors], ())
    sum_fc2, sum_fc1, sum_proj, sum_qkv, sum_vectors = (
        pipe.state for pipe in (put_fc2, put_fc1, put_proj, put_qkv, put_vectors)
    )
    new_qkv = adamw(sum_qkv, first_qkv, second_qkv, master_qkv, RATE_MATRIX, DECAY_MATRIX)
    new_proj = adamw(sum_proj, first_proj, second_proj, master_proj, RATE_MATRIX, DECAY_MATRIX)
    new_fc1 = adamw(sum_fc1, first_fc1, second_fc1, master_fc1, RATE_MATRIX, DECAY_MATRIX)
    new_fc2 = adamw(sum_fc2, first_fc2, second_fc2, master_fc2, RATE_MATRIX, DECAY_MATRIX)
    new_vectors = adamw(
        sum_vectors, first_vectors, second_vectors, master_vectors, RATE_VECTOR, 0.0
    )
    return (
        block_out,
        grad_input,
        sum_qkv,
        sum_proj,
        sum_fc1,
        sum_fc2,
        sum_vectors,
        new_qkv[0],
        new_proj[0],
        new_fc1[0],
        new_fc2[0],
        new_vectors[0],
        new_qkv[1],
        new_proj[1],
        new_fc1[1],
        new_fc2[1],
        new_vectors[1],
        new_qkv[2],
        new_proj[2],
        new_fc1[2],
        new_fc2[2],
        new_vectors[2],
    )


def solution(mesh):
    placed = (
        P(("dp", "zero"), None, None),
        P(("dp", "zero"), None, None),
        P(("dp", "zero")),
        P("zero", None),
        P("zero", None),
        P("zero", None),
        P("zero", None),
        P(None, "zero"),
        P("zero", None),
        P("zero", None),
        P("zero", None),
        P("zero", None),
        P(None, "zero"),
        P("zero", None),
        P("zero", None),
        P("zero", None),
        P("zero", None),
        P(None, "zero"),
    )
    return jax.shard_map(
        per_device,
        mesh=mesh,
        in_specs=placed,
        out_specs=(
            P(("dp", "zero"), None, None),
            P(("dp", "zero"), None, None),
            P("zero", None),
            P("zero", None),
            P("zero", None),
            P("zero", None),
            P(None, "zero"),
            P("zero", None),
            P("zero", None),
            P("zero", None),
            P("zero", None),
            P(None, "zero"),
            P("zero", None),
            P("zero", None),
            P("zero", None),
            P("zero", None),
            P(None, "zero"),
            P("zero", None),
            P("zero", None),
            P("zero", None),
            P("zero", None),
            P(None, "zero"),
        ),
        check_vma=False,
    )
```
